256 devices in a mesh: rep: 16 (over y_hi, z), row: 16 (over x, y_lo, core).
Axes of the slice: x: 4, y: 4 (y_hi: 2, y_lo: 2; y = y_hi * 2 + y_lo), z: 8, core: 2. Of those that a mesh axis runs over, the one named last changes fastest.
Arguments:
- features: bfloat16 [131072, 256], P(('rep', 'row')), may hold values from -6 to 6
- adj_values: bfloat16 [16, 16, 256, 128, 128], P('rep', 'row'), may hold values from -0.109375 to 0.109375
- block_rows: int32 [16, 16, 256], P('rep', 'row'), may hold values from 0 to 63, as said below
- block_cols: int32 [16, 16, 256], P('rep', 'row'), may hold values from 0 to 63
- counts: int32 [16, 16], P('rep', 'row'), may hold values from 42 to 256, as said below
- weight: bfloat16 [256, 256], replicated, may hold values from -0.375 to 0.375
- bias: float32 [256], replicated, may hold values from -3 to 3
- cotangent: bfloat16 [131072, 256], P(('rep', 'row')), may hold values from -6 to 6
Outputs:
- activations: bfloat16 [131072, 256], P(('rep', 'row'))
- grad_features: bfloat16 [131072, 256], P(('rep', 'row'))
- grad_weight: float32 [256, 256], replicated
- grad_bias: float32 [256], replicated
The draws below stay inside these ranges and needn't reach their ends.
Inputs may be any that keep to these rules, and one draw needn't show every extreme that they name: Within one device's list the pairs (block_rows, block_cols) are distinct, live or not. `counts`: the live entries are the first ones of each list; at least one list is full.
All inputs are finite; a program needn't handle non-finite values.
Results may differ from the reference program's by a relative error of at most 0.028.
Values may be sent and summed in bfloat16 or wider, within the bound.
A program may use at most 128 MiB of HBM per device.

```python
import jax
import jax.numpy as jnp
from jax import lax

F = 256
BS = 128
BLK_DEV = 4
RB = 64
CB = 64
CAP = 256
NODES = 131072
N_REP = 16
N_ROW = 16


def block_layout(key):
    device_keys = jax.random.split(key, N_REP * N_ROW)
    cell_ids = jax.vmap(lambda device_key: jax.random.permutation(device_key, RB * CB)[:CAP])(device_keys)
    return cell_ids.reshape(N_REP, N_ROW, CAP).astype(jnp.int32)


def draw_block_rows(key, part):
    return (block_layout(key) // CB).astype(jnp.int32)


def draw_block_cols(key, part):
    return (block_layout(key) % CB).astype(jnp.int32)


def draw_counts(key, part):
    key = jax.random.fold_in(key, 3)
    key_divisor, key_chosen = jax.random.split(key)
    divisor = jax.random.randint(key_divisor, (N_REP, N_ROW), 1, 7)
    base_counts = CAP // divisor
    chosen = jax.random.randint(key_chosen, (), 0, N_REP * N_ROW)
    flat_counts = base_counts.reshape(-1).at[chosen].set(CAP)
    return flat_counts.reshape(N_REP, N_ROW).astype(jnp.int32)


def steps_of(rng, dims, pieces, low, top_value):
    factor_of = 1.0
    for axis_at, shards_of in pieces:
        draws = jax.random.uniform(jax.random.fold_in(jax.random.fold_in(rng, 6), axis_at), (shards_of,), jnp.float32, low / len(pieces), top_value / len(pieces))
        factor_of = factor_of * jnp.repeat(jnp.exp(draws), dims[axis_at] // shards_of).reshape((-1,) + (1,) * (len(dims) - 1 - axis_at))
    return factor_of


def gaussian(stream_key, extent, spread, reach, shards=(), held_as=jnp.bfloat16):
    level = steps_of(stream_key, extent, shards, -0.22, 0.18) if shards else 1.0
    array = jax.random.normal(stream_key, extent, jnp.float32) * spread * level
    return jnp.minimum(jnp.maximum(array, -reach), reach).astype(held_as)


def setup_inputs(seed: int = 0) -> dict:
    seeds = jax.random.split(jax.random.key(seed), 9)
    return {
        "features": gaussian(seeds[0], (NODES, F), 1.0, 6.0, ((0, 256),)),
        "adj_values": gaussian(seeds[1], (N_REP, N_ROW, CAP, BS, BS), (BS * N_REP * CB // 40) ** -0.5, 0.109375, ((0, 16), (1, 16))),
        "block_rows": draw_block_rows(jax.random.fold_in(seeds[8], 71), 0),
        "block_cols": draw_block_cols(jax.random.fold_in(seeds[8], 71), 0),
        "counts": draw_counts(jax.random.fold_in(seeds[8], 71), 0),
        "weight": gaussian(seeds[5], (F, F), F ** -0.5, 0.375),
        "bias": gaussian(seeds[6], (F,), 0.5, 3.0, (), jnp.float32),
        "cotangent": gaussian(seeds[7], (NODES, F), 1.0, 6.0, ((0, 256),)),
    }


def silu_slope(pre_act):
    sig = jax.nn.sigmoid(pre_act)
    return sig * (1.0 + pre_act * (1.0 - sig))


def reference(features, adj_values, block_rows, block_cols, counts, weight, bias, cotangent):
    row_devs = CB // BLK_DEV
    all_devs = N_REP * N_ROW
    node_blocks = NODES // BS
    feat_blocks = features.astype(jnp.float32).reshape(node_blocks, BS, F)
    block_vals = adj_values.reshape(all_devs, CAP, BS, BS)
    row_local = block_rows.reshape(all_devs, CAP)
    col_local = block_cols.reshape(all_devs, CAP)
    live_count = counts.reshape(all_devs)
    device_ids = jnp.arange(all_devs, dtype=jnp.int32)
    rep_ids = device_ids // row_devs
    row_ids = device_ids % row_devs
    slot_ids = jnp.arange(CAP, dtype=jnp.int32)

    def global_rows(local, row_index):
        return ((local // BLK_DEV * row_devs + row_index) * BLK_DEV + local % BLK_DEV).astype(jnp.int32)

    def global_cols(local, rep_index):
        return ((rep_index * row_devs + local // BLK_DEV) * BLK_DEV + local % BLK_DEV).astype(jnp.int32)

    items = (block_vals, row_local, col_local, live_count, rep_ids, row_ids)

    def forward_step(running, device_item):
        vals_now, rows_now, cols_now, count_now, rep_index, row_index = device_item
        picked = feat_blocks[global_cols(cols_now, rep_index)]
        product = jnp.einsum("sij,sjf->sif", vals_now.astype(jnp.float32), picked)
        product = jnp.where((slot_ids < count_now)[:, None, None], product, 0.0)
        device_part = jnp.zeros((RB, BS, F), jnp.float32).at[rows_now].add(product)
        rounded = lax.optimization_barrier(device_part.astype(jnp.bfloat16)).astype(jnp.float32)
        destination = global_rows(jnp.arange(RB, dtype=jnp.int32), row_index)
        return running.at[destination].add(rounded), None

    summed, _ = lax.scan(forward_step, jnp.zeros((node_blocks, BS, F), jnp.float32), items)
    aggregated = summed.reshape(NODES, F).astype(jnp.bfloat16)
    pre_act = jnp.dot(aggregated, weight, preferred_element_type=jnp.float32) + bias
    activations = jax.nn.silu(pre_act).astype(jnp.bfloat16)
    grad_pre = (cotangent.astype(jnp.float32) * silu_slope(pre_act)).astype(jnp.bfloat16)
    grad_weight = jnp.dot(aggregated.T, grad_pre, preferred_element_type=jnp.float32)
    grad_bias = jnp.sum(grad_pre.astype(jnp.float32), axis=0)
    back_rows = jnp.dot(grad_pre, weight.T, preferred_element_type=jnp.float32).astype(jnp.bfloat16)
    back_blocks = back_rows.astype(jnp.float32).reshape(node_blocks, BS, F)

    def backward_step(running, device_item):
        vals_now, rows_now, cols_now, count_now, rep_index, row_index = device_item
        picked = back_blocks[global_rows(rows_now, row_index)]
        product = jnp.einsum("sji,sjf->sif", vals_now.astype(jnp.float32), picked)
        product = jnp.where((slot_ids < count_now)[:, None, None], product, 0.0)
        device_part = jnp.zeros((CB, BS, F), jnp.float32).at[cols_now].add(product)
        rounded = lax.optimization_barrier(device_part.astype(jnp.bfloat16)).astype(jnp.float32)
        destination = global_cols(jnp.arange(CB, dtype=jnp.int32), rep_index)
        return running.at[destination].add(rounded), None

    gathered, _ = lax.scan(backward_step, jnp.zeros((node_blocks, BS, F), jnp.float32), items)
    grad_features = gathered.reshape(NODES, F).astype(jnp.bfloat16)
    return (activations, grad_features, grad_weight, grad_bias)
```

```python
import functools

import jax
import jax.numpy as jnp
from jax import lax
from jax.experimental import pallas as pl
from jax.experimental.pallas import tpu as pltpu
from jax.sharding import PartitionSpec as P

MESH = pl.DeviceIdType.MESH
BF = jnp.bfloat16
F32 = jnp.float32
B = 128
CAP = 256
RB = 64
PAIRS = 160
NZ = 8
UNROLL = 20
VMEM_LIMIT = 58 * 2**20


def rem(a, n):
    return lax.rem(a, n)


def place():
    r = lax.axis_index("rep")
    i = lax.axis_index("row")
    return lax.div(r, 8), rem(r, 8), lax.div(i, 4), rem(lax.div(i, 2), 2), rem(i, 2)


def device(yh, z, x, yl, c):
    return (yh * 8 + z, x * 4 + yl * 2 + c)


class Links:
    def __init__(self, send_sem, recv_sem):
        self.send_sem, self.recv_sem, self.copies = send_sem, recv_sem, []

    def send(self, src, dst, to):
        k = len(self.copies)
        copy = pltpu.make_async_remote_copy(
            src_ref=src, dst_ref=dst, send_sem=self.send_sem.at[k], recv_sem=self.recv_sem.at[k],
            device_id=to, device_id_type=MESH,
        )
        copy.start()
        self.copies.append(copy)
        return copy

    def finish(self):
        for copy in self.copies:
            copy.wait_send()


def greet(partners):
    barrier = pltpu.get_barrier_semaphore()
    for to in partners:
        pl.semaphore_signal(barrier, inc=1, device_id=to, device_id_type=MESH)
    pl.semaphore_wait(barrier, len(partners))


def run(*tasks):
    tasks = list(tasks)
    while tasks:
        for task in list(tasks):
            if next(task, "end") == "end":
                tasks.remove(task)


def products(meta, base, adj, source, sums, adj_first):
    def step(t, acc):
        a0, a1 = adj[meta[base, t]], adj[meta[base + 1, t]]
        x0, x1 = source[meta[base + 2, t]], source[meta[base + 3, t]]
        if adj_first:
            left, right = jnp.concatenate([a0, a1], 1), jnp.concatenate([x0, x1], 0)
        else:
            left, right = jnp.concatenate([x0, x1], 1), jnp.concatenate([a0, a1], 0)
        term = jnp.dot(left, right, preferred_element_type=F32)
        acc = jnp.where(meta[base + 4, t] != 0, 0.0, acc) + term
        sums[t] = acc.astype(BF)
        return acc

    def group(g, acc):
        for k in range(UNROLL):
            acc = step(g * UNROLL + k, acc)
        return acc

    acc = jnp.zeros((B, B), F32)
    sums[PAIRS] = jnp.zeros((B, B), BF)
    for g in range(PAIRS // UNROLL):
        acc = lax.fori_loop(g, g + 1, group, acc)
        yield


def sort_kernel(count_ref, rows_ref, cols_ref, out_ref):
    live = (lax.broadcasted_iota(jnp.int32, (1, CAP), 1) < count_ref[0, 0]).astype(F32)
    sub = lax.broadcasted_iota(jnp.int32, (CAP, CAP), 0).astype(F32)
    lane = lax.broadcasted_iota(jnp.int32, (CAP, CAP), 1).astype(F32)
    eye = (sub == lane).astype(F32)
    rows = rows_ref[...].astype(F32)
    cols = cols_ref[...].astype(F32)

    def column(v):
        return jnp.sum(eye * v, axis=1, keepdims=True)

    def order(key, source):
        key = jnp.where(live > 0, key, 64.0)
        key_col = column(key)
        same = jnp.where(key_col == key, 1.0, 0.0)
        rank = jnp.sum(jnp.where(sub < lane, same, 0.0), axis=0, keepdims=True)
        p = sub[:RB]
        n = jnp.sum(jnp.where(p == key, 1.0, 0.0), axis=1, keepdims=True)
        pairs = jnp.floor((n + 1.0) * 0.5)
        base = jnp.sum(jnp.where(p < key, pairs, 0.0), axis=0, keepdims=True)
        slot = jnp.where(live > 0, 2.0 * base + rank, -1.0)
        slot_col = column(slot)
        first_hot = jnp.where(slot_col == 2.0 * lane, 1.0, 0.0)
        second_hot = jnp.where(slot_col == 2.0 * lane + 1.0, 1.0, 0.0)
        source_col = column(source)
        fresh_col = column(jnp.where(rank == 0.0, 1.0, 0.0))

        def pick(hot, v):
            return jnp.sum(hot * v, axis=0, keepdims=True)

        entry = sub[:, :1]
        a0 = pick(first_hot, entry - CAP) + CAP
        a1 = pick(second_hot, entry - CAP) + CAP
        before = jnp.sum(jnp.where(p < lane[:RB], pairs, 0.0), axis=0, keepdims=True)
        mine = jnp.sum(jnp.where(p == lane[:RB], pairs, 0.0), axis=0, keepdims=True)
        last = jnp.where(mine > 0, before + mine - 1.0, float(PAIRS))
        zero = jnp.zeros((1, CAP), F32)
        return [a0, a1, pick(first_hot, source_col), pick(second_hot, source_col), pick(first_hot, fresh_col), last, zero, zero]

    i = jnp.floor(cols * 0.25)
    x = jnp.floor(i * 0.25)
    yl = jnp.floor((i - 4.0 * x) * 0.5)
    c = i - 4.0 * x - 2.0 * yl
    col_place = (c * 8.0 + x * 2.0 + yl) * 4.0 + (cols - 4.0 * i)
    j = jnp.floor(rows * 0.25)
    k = rows - 4.0 * j
    part = jnp.floor(k * 0.5)
    row_place = part * 32.0 + j * 2.0 + (k - 2.0 * part)
    table = order(rows, col_place) + order(cols, row_place)
    out_ref[...] = jnp.concatenate(table, axis=0).astype(jnp.int32)


def sort_lists(count, rows, cols):
    return pl.pallas_call(
        sort_kernel,
        out_shape=jax.ShapeDtypeStruct((16, CAP), jnp.int32),
        in_specs=[
            pl.BlockSpec(memory_space=pltpu.SMEM),
            pl.BlockSpec(memory_space=pltpu.VMEM),
            pl.BlockSpec(memory_space=pltpu.VMEM),
        ],
        out_specs=pl.BlockSpec(memory_space=pltpu.VMEM),
    )(count, rows, cols)


def gather_row(links, panel):
    yh, z, x, yl, c = place()
    xp, xm, yo, co = rem(x + 1, 4), rem(x + 3, 4), 1 - yl, 1 - c

    def one(at_x, at_y):
        return panel.at[pl.ds((c * 8 + at_x * 2 + at_y) * 4, 4)]

    def two(at_x):
        return panel.at[pl.ds((c * 8 + at_x * 2) * 4, 8)]

    right, left = device(yh, z, xp, yl, c), device(yh, z, xm, yl, c)
    over_y, sibling = device(yh, z, x, yo, c), device(yh, z, x, yl, co)
    mine, other = one(x, yl), one(x, yo)
    y_copy = links.send(mine, mine, over_y)
    r_mine = links.send(mine, mine, right)
    l_mine = links.send(mine, mine, left)
    to_core = [links.send(mine, mine, sibling)]
    yield
    y_copy.wait_recv()
    r_other = links.send(other, other, right)
    l_other = links.send(other, other, left)
    to_core.append(links.send(other, other, sibling))
    yield
    r_mine.wait_recv()
    r_far = links.send(one(xm, yl), one(xm, yl), right)
    yield
    l_other.wait_recv()
    l_far = links.send(one(xp, yo), one(xp, yo), left)
    yield
    r_other.wait_recv()
    to_core.append(links.send(two(xm), two(xm), sibling))
    l_mine.wait_recv()
    to_core.append(links.send(two(xp), two(xp), sibling))
    yield
    far = rem(x + 2, 4)
    r_far.wait_recv()
    to_core.append(links.send(one(far, yl), one(far, yl), sibling))
    l_far.wait_recv()
    to_core.append(links.send(one(far, yo), one(far, yo), sibling))
    yield
    for copy in to_core:
        copy.wait_recv()


def total(*terms):
    out = terms[0].astype(F32)
    for term in terms[1:]:
        out = out + term.astype(F32)
    return out


def own_rows(meta, sums, yh, z, o, block):
    p = (yh * 8 + rem(z + o, NZ)) * 4 + block
    return sums[meta[5, p]]


NEED = (4, 5, 3, 6, 2, 7, 1, 0)


def reduce_rep_a(links, meta, sums, ys, yr, ar, al, agg, h):
    yh, z, x, yl, c = place()
    up, down = device(yh, rem(z + 1, NZ), x, yl, c), device(yh, rem(z + NZ - 1, NZ), x, yl, c)
    over = device(1 - yh, z, x, yl, c)
    y_copies = []
    for g in range(4):
        for n in (2 * g, 2 * g + 1):
            for k in range(2):
                ys[n, k] = own_rows(meta, sums, 1 - yh, z, NEED[n], k)
        part = pl.ds(2 * g, 2)
        y_copies.append(links.send(ys.at[part], yr.at[part], over))
    yield
    up_copy = down_copy = None
    for s in range(5):
        if s < 4:
            y_copies[s].wait_recv()
        if s > 0:
            up_copy.wait_recv()
        if s < 4:
            n = NEED.index(4 - s)
            for k in range(2):
                terms = [own_rows(meta, sums, yh, z, 4 - s, k), yr[n, k]]
                if s > 0:
                    terms.append(ar[s, k])
                ar[s, k] = total(*terms).astype(BF)
            up_copy = links.send(ar.at[s], ar.at[s + 1], up)
        if s > 0 and s < 4:
            down_copy.wait_recv()
        if s < 3:
            n = NEED.index(5 + s)
            for k in range(2):
                terms = [own_rows(meta, sums, yh, z, 5 + s, k), yr[n, k]]
                if s > 0:
                    terms.append(al[s, k])
                al[s, k] = total(*terms).astype(BF)
            down_copy = links.send(al.at[s], al.at[s + 1], down)
        yield
    n = NEED.index(0)
    for k in range(2):
        agg[pl.ds(k * B, B), pl.ds(h * B, B)] = total(
            own_rows(meta, sums, yh, z, 0, k), yr[n, k], ar[4, k], al[3, k]
        ).astype(BF)


def reduce_rep_b(links, meta, sums, br, bl, by, agg, h):
    yh, z, x, yl, c = place()
    up, down = device(yh, rem(z + 1, NZ), x, yl, c), device(yh, rem(z + NZ - 1, NZ), x, yl, c)
    over = device(1 - yh, z, x, yl, c)
    sides = (yh, 1 - yh)
    up_copy = down_copy = None
    for s in range(5):
        if s > 0:
            down_copy.wait_recv()
        if s < 4:
            for n in range(2):
                for k in range(2):
                    terms = [own_rows(meta, sums, sides[n], z, 4 + s, 2 + k)]
                    if s > 0:
                        terms.append(bl[s, n, k])
                    bl[s, n, k] = total(*terms).astype(BF)
            down_copy = links.send(bl.at[s], bl.at[s + 1], down)
        if s > 0 and s < 4:
            up_copy.wait_recv()
        if s < 3:
            for n in range(2):
                for k in range(2):
                    terms = [own_rows(meta, sums, sides[n], z, 3 - s, 2 + k)]
                    if s > 0:
                        terms.append(br[s, n, k])
                    br[s, n, k] = total(*terms).astype(BF)
            up_copy = links.send(br.at[s], br.at[s + 1], up)
        yield
    for k in range(2):
        by[0, k] = total(own_rows(meta, sums, 1 - yh, z, 0, 2 + k), bl[4, 1, k], br[3, 1, k]).astype(BF)
    y_copy = links.send(by.at[0], by.at[1], over)
    yield
    y_copy.wait_recv()
    for k in range(2):
        agg[pl.ds((2 + k) * B, B), pl.ds(h * B, B)] = total(
            own_rows(meta, sums, yh, z, 0, 2 + k), bl[4, 0, k], br[3, 0, k], by[1, k]
        ).astype(BF)


def chain(*tasks):
    for task in tasks:
        yield from task


def together(*tasks):
    tasks = list(tasks)
    while tasks:
        for task in list(tasks):
            if next(task, "end") == "end":
                tasks.remove(task)
            else:
                yield


FWD_COPIES = 64
FWD_SCRATCH = [
    (RB, B, B), (PAIRS + 1, B, B), (8, 2, B, B), (8, 2, B, B), (5, 2, B, B), (4, 2, B, B),
    (4, 2, 2, B, B), (5, 2, 2, B, B), (2, 2, B, B),
]


def fwd_kernel(meta, feat, adj_hbm, agg, adj, *rest):
    halves = [rest[:9], rest[9:18]]
    send_sem, recv_sem, local_sem = rest[18:]
    yh, z, x, yl, c = place()
    links = Links(send_sem, recv_sem)
    adj_copy = pltpu.make_async_copy(adj_hbm, adj.at[pl.ds(0, CAP)], local_sem)
    adj_copy.start()
    adj[CAP] = jnp.zeros((B, B), BF)
    slot = (c * 8 + x * 2 + yl) * 4
    for h in range(2):
        for k in range(4):
            halves[h][0][slot + k] = feat[pl.ds(k * B, B), pl.ds(h * B, B)]
    greet([
        device(yh, z, rem(x + 1, 4), yl, c), device(yh, z, rem(x + 3, 4), yl, c),
        device(yh, z, x, 1 - yl, c), device(yh, z, x, yl, 1 - c), device(1 - yh, z, x, yl, c),
        device(yh, rem(z + 1, NZ), x, yl, c), device(yh, rem(z + NZ - 1, NZ), x, yl, c),
    ])
    gathers = [gather_row(links, halves[h][0]) for h in range(2)]
    for _ in range(3):
        next(gathers[0])
    next(gathers[1])
    run(gathers[0])
    adj_copy.wait()
    panel, sums = halves[0][0], halves[0][1]
    run(products(meta, 0, adj, panel, sums, True), gathers[1])

    def reduces(h):
        panel, sums, ys, yr, ar, al, br, bl, by = halves[h]
        return (
            reduce_rep_b(links, meta, sums, br, bl, by, agg, h),
            reduce_rep_a(links, meta, sums, ys, yr, ar, al, agg, h),
        )

    first = reduces(0)
    for task in first:
        next(task)
    panel, sums = halves[1][0], halves[1][1]
    work = products(meta, 0, adj, panel, sums, True)
    turn = together(*first)
    while next(work, "end") != "end":
        next(turn, None)
    second = reduces(1)
    run(turn, *second)
    links.finish()


def forward(meta, feat, adj):
    return pl.pallas_call(
        fwd_kernel,
        out_shape=jax.ShapeDtypeStruct((512, 256), BF),
        in_specs=[
            pl.BlockSpec(memory_space=pltpu.SMEM),
            pl.BlockSpec(memory_space=pltpu.VMEM),
            pl.BlockSpec(memory_space=pl.ANY),
        ],
        out_specs=pl.BlockSpec(memory_space=pltpu.VMEM),
        scratch_shapes=[pltpu.VMEM((CAP + 1, B, B), BF)]
        + [pltpu.VMEM(shape, BF) for shape in FWD_SCRATCH * 2]
        + [pltpu.SemaphoreType.DMA((FWD_COPIES,)), pltpu.SemaphoreType.DMA((FWD_COPIES,)), pltpu.SemaphoreType.DMA],
        compiler_params=pltpu.CompilerParams(collective_id=1, has_side_effects=True, vmem_limit_bytes=VMEM_LIMIT),
    )(meta, feat, adj)


def gather_rep_a(links, panel):
    yh, z, x, yl, c = place()
    up, down = device(yh, rem(z + 1, NZ), x, yl, c), device(yh, rem(z + NZ - 1, NZ), x, yl, c)
    over = device(1 - yh, z, x, yl, c)

    def at(o):
        return panel.at[pl.ds((yh * 8 + rem(z + NZ + o, NZ)) * 2, 2)]

    up_copy = links.send(at(0), at(0), up)
    down_copy = links.send(at(0), at(0), down)
    y_copies = [links.send(at(0), at(0), over)]
    yield
    for s in range(1, 5):
        up_copy.wait_recv()
        if s < 4:
            up_copy = links.send(at(-s), at(-s), up)
        y_copies.append(links.send(at(-s), at(-s), over))
        if s < 4:
            down_copy.wait_recv()
            if s < 3:
                down_copy = links.send(at(s), at(s), down)
            y_copies.append(links.send(at(s), at(s), over))
        yield
    for copy in y_copies:
        copy.wait_recv()


def gather_rep_b(links, panel):
    yh, z, x, yl, c = place()
    up, down = device(yh, rem(z + 1, NZ), x, yl, c), device(yh, rem(z + NZ - 1, NZ), x, yl, c)
    over = device(1 - yh, z, x, yl, c)

    def at(side, o):
        return panel.at[pl.ds(32 + (side * 8 + rem(z + NZ + o, NZ)) * 2, 2)]

    y_copy = links.send(at(yh, 0), at(yh, 0), over)
    ups, downs = [None, None], [None, None]
    sides = (yh, 1 - yh)
    for s in range(0, 5):
        for n in range(2):
            if s == 0 and n == 1:
                yield
                y_copy.wait_recv()
            if s > 0:
                downs[n].wait_recv()
            if s < 4:
                downs[n] = links.send(at(sides[n], s), at(sides[n], s), down)
            if s > 0 and s < 4:
                ups[n].wait_recv()
            if s < 3:
                ups[n] = links.send(at(sides[n], -s), at(sides[n], -s), up)
        yield


ORDER = ((2, 0), (2, 1), (1, 0), (3, 1), (1, 1), (3, 0), (0, 1), (0, 0))


def reduce_row(links, meta, sums, cs, cr, stage, got, result, h):
    yh, z, x, yl, c = place()
    right, left = device(yh, z, rem(x + 1, 4), yl, c), device(yh, z, rem(x + 3, 4), yl, c)
    over_y, sibling = device(yh, z, x, 1 - yl, c), device(yh, z, x, yl, 1 - c)

    def own(core, dx, other, k):
        side = 1 - yl if other else yl
        q = (rem(x + dx, 4) * 4 + side * 2 + core) * 4 + k
        return sums[meta[13, q]]

    core_copies = []
    for g in range(4):
        for n in (2 * g, 2 * g + 1):
            for k in range(4):
                cs[n, k] = own(1 - c, *ORDER[n], k)
        part = pl.ds(2 * g, 2)
        core_copies.append(links.send(cs.at[part], cr.at[part], sibling))

    def put(dst, dx, other, *more):
        n = ORDER.index((dx, other))
        for k in range(4):
            dst[k] = total(own(c, dx, other, k), cr[n, k], *[ref[k] for ref in more]).astype(BF)

    yield
    core_copies[0].wait_recv()
    put(stage.at[0], 2, 0)
    r_own1 = links.send(stage.at[0], got.at[0], right)
    put(stage.at[1], 2, 1)
    l_par1 = links.send(stage.at[1], got.at[1], left)
    core_copies[1].wait_recv()
    core_copies[2].wait_recv()
    put(stage.at[2], 1, 1)
    r_par = links.send(stage.at[2], got.at[2], right)
    put(stage.at[3], 3, 0)
    l_own = links.send(stage.at[3], got.at[3], left)
    yield
    r_own1.wait_recv()
    put(stage.at[4], 1, 0, got.at[0])
    r_own2 = links.send(stage.at[4], got.at[4], right)
    l_par1.wait_recv()
    put(stage.at[5], 3, 1, got.at[1])
    l_par2 = links.send(stage.at[5], got.at[5], left)
    core_copies[3].wait_recv()
    yield
    r_par.wait_recv()
    l_par2.wait_recv()
    put(stage.at[6], 0, 1, got.at[2], got.at[5])
    y_copy = links.send(stage.at[6], got.at[6], over_y)
    yield
    l_own.wait_recv()
    r_own2.wait_recv()
    y_copy.wait_recv()
    n = ORDER.index((0, 0))
    for k in range(4):
        out = total(own(c, 0, 0, k), cr[n, k], got[3, k], got[4, k], got[6, k])
        result[pl.ds(k * B, B), pl.ds(h * B, B)] = out.T.astype(BF)


def reduce_weight(links, pieces, core_in, x_in, y_in, z_in, s1, s2, out):
    yh, z, x, yl, c = place()
    y = yh * 2 + yl

    def at_y(v):
        return device(lax.div(v, 2), z, x, rem(v, 2), c)

    half = pl.ds((1 - c) * 16, 16)
    copy = links.send(pieces.at[half], core_in, device(yh, z, x, yl, 1 - c))
    yield
    copy.wait_recv()
    s1[...] = pieces[pl.ds(c * 16, 16)] + core_in[...]
    copies = []
    for d in range(1, 4):
        to = rem(x + d, 4)
        copies.append(links.send(s1.at[pl.ds(to * 4, 4)], x_in.at[d - 1], device(yh, z, to, yl, c)))
    yield
    for copy in copies:
        copy.wait_recv()
    s2[...] = s1[pl.ds(x * 4, 4)] + x_in[0] + x_in[1] + x_in[2]
    copies = []
    for d in range(1, 4):
        to = rem(y + d, 4)
        copies.append(links.send(s2.at[to], y_in.at[d - 1], at_y(to)))
    yield
    for copy in copies:
        copy.wait_recv()
    z_in[z] = s2[y] + y_in[0] + y_in[1] + y_in[2]
    copies = []
    for d in range(1, NZ):
        copies.append(links.send(z_in.at[z], z_in.at[z], device(yh, rem(z + d, NZ), x, yl, c)))
    yield
    for copy in copies:
        copy.wait_recv()
    summed = z_in[0]
    for n in range(1, NZ):
        summed = summed + z_in[n]
    spot = c * 16 + x * 4 + y
    out[spot] = summed
    copies = [links.send(out.at[spot], out.at[spot], at_y(rem(y + d, 4))) for d in range(1, 4)]
    yield
    for copy in copies:
        copy.wait_recv()
    spots = pl.ds(c * 16 + x * 4, 4)
    copies = [links.send(out.at[spots], out.at[spots], device(yh, z, rem(x + d, 4), yl, c)) for d in range(1, 4)]
    yield
    for copy in copies:
        copy.wait_recv()
    spots = pl.ds(c * 16, 16)
    copy = links.send(out.at[spots], out.at[spots], device(yh, z, x, yl, 1 - c))
    yield
    copy.wait_recv()


BWD_COPIES = 112
BWD_SCRATCH = [(RB, B, B), (PAIRS + 1, B, B), (8, 4, B, B), (8, 4, B, B), (7, 4, B, B), (7, 4, B, B)]


def bwd_kernel(meta, agg, cot, weight, bias, adj_hbm, act, result, gw, gb, adj, *rest):
    halves = [rest[:6], rest[6:12]]
    pieces, core_in, x_in, y_in, z_in, s1, s2, out, grad, send_sem, recv_sem, local_sem = rest[12:]
    yh, z, x, yl, c = place()
    links = Links(send_sem, recv_sem)
    adj_copy = pltpu.make_async_copy(adj_hbm, adj.at[pl.ds(0, CAP)], local_sem)
    adj_copy.start()
    adj[CAP] = jnp.zeros((B, B), BF)
    spot = (yh * 8 + z) * 2
    for k in range(4):
        rows = pl.ds(k * B, B)
        pre = jnp.dot(agg[rows, :], weight[...], preferred_element_type=F32) + bias[...]
        s = jax.nn.sigmoid(pre)
        act[rows, :] = (pre * s).astype(BF)
        grad_pre = (cot[rows, :].astype(F32) * (s * (1.0 + pre * (1.0 - s)))).astype(BF)
        grad[rows, :] = grad_pre
        back = lax.dot_general(weight[...], grad_pre, (((1,), (1,)), ((), ())), preferred_element_type=F32).astype(BF)
        for h in range(2):
            halves[h][0][(k // 2) * 32 + spot + k % 2] = back[h * B : (h + 1) * B]
    greet(
        [device(yh, rem(z + d, NZ), x, yl, c) for d in range(1, NZ)]
        + [device(yh, z, rem(x + d, 4), yl, c) for d in range(1, 4)]
        + [device(yh, z, x, 1 - yl, c), device(1 - yh, z, x, yl, c), device(1 - yh, z, x, 1 - yl, c)]
        + [device(yh, z, x, yl, 1 - c)]
    )
    gathers = [together(gather_rep_b(links, halves[h][0]), gather_rep_a(links, halves[h][0])) for h in range(2)]
    for _ in range(4):
        next(gathers[0])

    gw_local = lax.dot_general(agg[...], grad[...], (((0,), (0,)), ((), ())), preferred_element_type=F32)
    gb_local = jnp.sum(grad[...].astype(F32), axis=0, keepdims=True)
    row = lax.broadcasted_iota(jnp.int32, (8, B), 0)
    bias_tile = jnp.where(row == 0, gb_local[:, :B], jnp.where(row == 1, gb_local[:, B:], 0.0))
    for n in range(32):
        pieces[n, :, 0:256] = gw_local[n * 8 : n * 8 + 8]
        pieces[n, :, 256:384] = bias_tile
    weights = reduce_weight(links, pieces, core_in, x_in, y_in, z_in, s1, s2, out)
    next(weights)
    run(gathers[0], gathers[1], weights)
    adj_copy.wait()
    panel, sums = halves[0][0], halves[0][1]
    run(products(meta, 8, adj, panel, sums, False))

    def reduces(h):
        panel, sums, cs, cr, stage, got = halves[h]
        return reduce_row(links, meta, sums, cs, cr, stage, got, result, h)

    first = reduces(0)
    next(first)
    panel, sums = halves[1][0], halves[1][1]
    run(products(meta, 8, adj, panel, sums, False), first)
    run(reduces(1))
    for n in range(32):
        gw[n * 8 : n * 8 + 8, :] = out[n, :, 0:256]
    gb[:, 0:B] = out[0, 0:1, 256:384]
    gb[:, B:256] = out[0, 1:2, 256:384]
    links.finish()


def backward(meta, agg, cot, weight, bias, adj):
    vmem = pl.BlockSpec(memory_space=pltpu.VMEM)
    return pl.pallas_call(
        bwd_kernel,
        out_shape=(
            jax.ShapeDtypeStruct((512, 256), BF),
            jax.ShapeDtypeStruct((512, 256), BF),
            jax.ShapeDtypeStruct((256, 256), F32),
            jax.ShapeDtypeStruct((1, 256), F32),
        ),
        in_specs=[pl.BlockSpec(memory_space=pltpu.SMEM), vmem, vmem, vmem, vmem, pl.BlockSpec(memory_space=pl.ANY)],
        out_specs=(vmem, vmem, vmem, vmem),
        scratch_shapes=[pltpu.VMEM((CAP + 1, B, B), BF)]
        + [pltpu.VMEM(shape, BF) for shape in BWD_SCRATCH * 2]
        + [
            pltpu.VMEM(shape, F32)
            for shape in [(32, 8, 384), (16, 8, 384), (3, 4, 8, 384), (3, 8, 384), (8, 8, 384), (16, 8, 384), (4, 8, 384), (32, 8, 384)]
        ]
        + [
            pltpu.VMEM((512, 256), BF),
            pltpu.SemaphoreType.DMA((BWD_COPIES,)),
            pltpu.SemaphoreType.DMA((BWD_COPIES,)),
            pltpu.SemaphoreType.DMA,
        ],
        compiler_params=pltpu.CompilerParams(collective_id=2, has_side_effects=True, vmem_limit_bytes=VMEM_LIMIT),
    )(meta, agg, cot, weight, bias, adj)


def per_device(features, adj_values, block_rows, block_cols, counts, weight, bias, cotangent):
    adj = adj_values.reshape(CAP, B, B)
    meta = sort_lists(counts, block_rows.reshape(1, CAP), block_cols.reshape(1, CAP))
    agg = forward(meta, features, adj)
    act, result, gw, gb = backward(meta, agg, cotangent, weight, bias.reshape(1, 256), adj)
    return act, result, gw, gb.reshape(256)


def solution(mesh):
    return jax.shard_map(
        per_device,
        mesh=mesh,
        in_specs=(
            P(("rep", "row"), None),
            P("rep", "row", None, None, None),
            P("rep", "row", None),
            P("rep", "row", None),
            P("rep", "row"),
            P(),
            P(),
            P(("rep", "row"), None),
        ),
        out_specs=(P(("rep", "row"), None), P(("rep", "row"), None), P(), P()),
        check_vma=False,
    )
```

```python
import functools

import jax
import jax.numpy as jnp
from jax import lax
from jax.experimental import pallas as pl
from jax.experimental.pallas import tpu as pltpu
from jax.sharding import PartitionSpec as P

MESH = pl.DeviceIdType.MESH
BF = jnp.bfloat16
F32 = jnp.float32
B = 128
CAP = 256
RB = 64
PAIRS = 160
NZ = 8
UNROLL = 20
VMEM_LIMIT = 58 * 2**20


def rem(a, n):
    return lax.rem(a, n)


def place():
    r = lax.axis_index("rep")
    i = lax.axis_index("row")
    return lax.div(r, 8), rem(r, 8), lax.div(i, 4), rem(lax.div(i, 2), 2), rem(i, 2)


def device(yh, z, x, yl, c):
    return (yh * 8 + z, x * 4 + yl * 2 + c)


class Links:
    def __init__(self, send_sem, recv_sem):
        self.send_sem, self.recv_sem, self.copies = send_sem, recv_sem, []

    def send(self, src, dst, to):
        k = len(self.copies)
        copy = pltpu.make_async_remote_copy(
            src_ref=src, dst_ref=dst, send_sem=self.send_sem.at[k], recv_sem=self.recv_sem.at[k],
            device_id=to, device_id_type=MESH,
        )
        copy.start()
        self.copies.append(copy)
        return copy

    def finish(self):
        for copy in self.copies:
            copy.wait_send()


def run(*tasks):
    tasks = list(tasks)
    while tasks:
        for task in list(tasks):
            if next(task, "end") == "end":
                tasks.remove(task)


def together(*tasks):
    tasks = list(tasks)
    while tasks:
        for task in list(tasks):
            if next(task, "end") == "end":
                tasks.remove(task)
            else:
                yield


def advance(task, n):
    for _ in range(n):
        next(task, None)


def products(meta, base, adj, source, sums, adj_first):
    def step(t, acc):
        a0, a1 = adj[meta[base, t]], adj[meta[base + 1, t]]
        x0, x1 = source[meta[base + 2, t]], source[meta[base + 3, t]]
        if adj_first:
            left, right = jnp.concatenate([a0, a1], 1), jnp.concatenate([x0, x1], 0)
        else:
            left, right = jnp.concatenate([x0, x1], 1), jnp.concatenate([a0, a1], 0)
        term = jnp.dot(left, right, preferred_element_type=F32)
        acc = jnp.where(meta[base + 4, t] != 0, 0.0, acc) + term
        sums[t] = acc.astype(BF)
        return acc

    def group(g, acc):
        for k in range(UNROLL):
            acc = step(g * UNROLL + k, acc)
        return acc

    acc = jnp.zeros((B, B), F32)
    sums[PAIRS] = jnp.zeros((B, B), BF)
    for g in range(PAIRS // UNROLL):
        acc = lax.fori_loop(g, g + 1, group, acc)
        yield


def sort_kernel(count_ref, rows_ref, cols_ref, out_ref):
    live = (lax.broadcasted_iota(jnp.int32, (1, CAP), 1) < count_ref[0, 0]).astype(F32)
    sub = lax.broadcasted_iota(jnp.int32, (CAP, CAP), 0).astype(F32)
    lane = lax.broadcasted_iota(jnp.int32, (CAP, CAP), 1).astype(F32)
    eye = (sub == lane).astype(F32)
    rows = rows_ref[...].astype(F32)
    cols = cols_ref[...].astype(F32)

    def column(v):
        return jnp.sum(eye * v, axis=1, keepdims=True)

    def order(key, source):
        key = jnp.where(live > 0, key, 64.0)
        key_col = column(key)
        same = jnp.where(key_col == key, 1.0, 0.0)
        rank = jnp.sum(jnp.where(sub < lane, same, 0.0), axis=0, keepdims=True)
        p = sub[:RB]
        n = jnp.sum(jnp.where(p == key, 1.0, 0.0), axis=1, keepdims=True)
        pairs = jnp.floor((n + 1.0) * 0.5)
        base = jnp.sum(jnp.where(p < key, pairs, 0.0), axis=0, keepdims=True)
        slot = jnp.where(live > 0, 2.0 * base + rank, -1.0)
        slot_col = column(slot)
        first_hot = jnp.where(slot_col == 2.0 * lane, 1.0, 0.0)
        second_hot = jnp.where(slot_col == 2.0 * lane + 1.0, 1.0, 0.0)
        source_col = column(source)
        fresh_col = column(jnp.where(rank == 0.0, 1.0, 0.0))

        def pick(hot, v):
            return jnp.sum(hot * v, axis=0, keepdims=True)

        entry = sub[:, :1]
        a0 = pick(first_hot, entry - CAP) + CAP
        a1 = pick(second_hot, entry - CAP) + CAP
        before = jnp.sum(jnp.where(p < lane[:RB], pairs, 0.0), axis=0, keepdims=True)
        mine = jnp.sum(jnp.where(p == lane[:RB], pairs, 0.0), axis=0, keepdims=True)
        last = jnp.where(mine > 0, before + mine - 1.0, float(PAIRS))
        zero = jnp.zeros((1, CAP), F32)
        return [a0, a1, pick(first_hot, source_col), pick(second_hot, source_col), pick(first_hot, fresh_col), last, zero, zero]

    i = jnp.floor(cols * 0.25)
    x = jnp.floor(i * 0.25)
    yl = jnp.floor((i - 4.0 * x) * 0.5)
    c = i - 4.0 * x - 2.0 * yl
    col_place = (c * 8.0 + x * 2.0 + yl) * 4.0 + (cols - 4.0 * i)
    table = order(rows, col_place) + order(cols, rows)
    out_ref[...] = jnp.concatenate(table, axis=0).astype(jnp.int32)


def sort_lists(count, rows, cols):
    return pl.pallas_call(
        sort_kernel,
        out_shape=jax.ShapeDtypeStruct((16, CAP), jnp.int32),
        in_specs=[
            pl.BlockSpec(memory_space=pltpu.SMEM),
            pl.BlockSpec(memory_space=pltpu.VMEM),
            pl.BlockSpec(memory_space=pltpu.VMEM),
        ],
        out_specs=pl.BlockSpec(memory_space=pltpu.VMEM),
    )(count, rows, cols)


def gather_row_first(links, panel):
    yh, z, x, yl, c = place()
    xp, xm, xf, yo = rem(x + 1, 4), rem(x + 3, 4), rem(x + 2, 4), 1 - yl

    def at(at_x, at_y, first, n):
        return panel.at[pl.ds((c * 8 + at_x * 2 + at_y) * 4 + first, n)]

    over_y, sibling = device(yh, z, x, yo, c), device(yh, z, x, yl, 1 - c)
    around = [device(yh, z, xp, yl, c), device(yh, z, xm, yl, c), device(yh, z, xf, yl, c)]
    origin = (xm, xp, xf)

    def send(at_x, at_y, first, n, to):
        ref = at(at_x, at_y, first, n)
        return links.send(ref, ref, to)

    y_lo = send(x, yl, 0, 2, over_y)
    hi = [send(x, yl, 2, 2, to) for to in around]
    y_hi = send(x, yl, 2, 2, over_y)
    lo = [send(x, yl, 0, 2, to) for to in around]
    to_core = [send(x, yl, 0, 4, sibling)]
    yield
    y_lo.wait_recv()
    lo_other = [send(x, yo, 0, 2, to) for to in around]
    hi_other = []
    for n in range(3):
        hi[n].wait_recv()
        hi_other.append(send(origin[n], yl, 2, 2, over_y))
    yield
    y_hi.wait_recv()
    to_core.append(send(x, yo, 0, 4, sibling))
    for n in range(3):
        lo[n].wait_recv()
        to_core.append(send(origin[n], yl, 0, 4, sibling))
    yield
    for n in range(3):
        lo_other[n].wait_recv()
        hi_other[n].wait_recv()
        to_core.append(send(origin[n], yo, 0, 4, sibling))
    yield
    for copy in to_core:
        copy.wait_recv()


def gather_row(links, panel):
    yh, z, x, yl, c = place()
    xp, xm, yo, co = rem(x + 1, 4), rem(x + 3, 4), 1 - yl, 1 - c

    def one(at_x, at_y):
        return panel.at[pl.ds((c * 8 + at_x * 2 + at_y) * 4, 4)]

    def two(at_x):
        return panel.at[pl.ds((c * 8 + at_x * 2) * 4, 8)]

    right, left = device(yh, z, xp, yl, c), device(yh, z, xm, yl, c)
    over_y, sibling = device(yh, z, x, yo, c), device(yh, z, x, yl, co)
    mine, other = one(x, yl), one(x, yo)
    y_copy = links.send(mine, mine, over_y)
    r_mine = links.send(mine, mine, right)
    l_mine = links.send(mine, mine, left)
    to_core = [links.send(mine, mine, sibling)]
    yield
    y_copy.wait_recv()
    r_other = links.send(other, other, right)
    l_other = links.send(other, other, left)
    to_core.append(links.send(other, other, sibling))
    r_mine.wait_recv()
    r_far = links.send(one(xm, yl), one(xm, yl), right)
    yield
    l_other.wait_recv()
    l_far = links.send(one(xp, yo), one(xp, yo), left)
    r_other.wait_recv()
    to_core.append(links.send(two(xm), two(xm), sibling))
    l_mine.wait_recv()
    to_core.append(links.send(two(xp), two(xp), sibling))
    yield
    far = rem(x + 2, 4)
    r_far.wait_recv()
    to_core.append(links.send(one(far, yl), one(far, yl), sibling))
    l_far.wait_recv()
    to_core.append(links.send(one(far, yo), one(far, yo), sibling))
    yield
    for copy in to_core:
        copy.wait_recv()


def total(*terms):
    out = terms[0].astype(F32)
    for term in terms[1:]:
        out = out + term.astype(F32)
    return out


def own_rows(meta, sums, yh, z, o, block):
    p = (yh * 8 + rem(z + o, NZ)) * 4 + block
    return sums[meta[5, p]]


NEED = (4, 5, 3, 6, 2, 7, 1, 0)


def reduce_rep_a(links, meta, sums, ys, yr, ar, al, agg, h):
    yh, z, x, yl, c = place()
    up, down = device(yh, rem(z + 1, NZ), x, yl, c), device(yh, rem(z + NZ - 1, NZ), x, yl, c)
    over = device(1 - yh, z, x, yl, c)
    blocks = range(A_BLOCKS[h])
    y_copies = []
    for g in range(4):
        for n in (2 * g, 2 * g + 1):
            for k in blocks:
                ys[n, k] = own_rows(meta, sums, 1 - yh, z, NEED[n], k)
        part = pl.ds(2 * g, 2)
        y_copies.append(links.send(ys.at[part], yr.at[part], over))
    yield
    up_copy = down_copy = None
    for s in range(5):
        if s < 4:
            y_copies[s].wait_recv()
        if s > 0:
            up_copy.wait_recv()
        if s < 4:
            n = NEED.index(4 - s)
            for k in blocks:
                terms = [own_rows(meta, sums, yh, z, 4 - s, k), yr[n, k]]
                if s > 0:
                    terms.append(ar[s, k])
                ar[s, k] = total(*terms).astype(BF)
            up_copy = links.send(ar.at[s], ar.at[s + 1], up)
        if s > 0 and s < 4:
            down_copy.wait_recv()
        if s < 3:
            n = NEED.index(5 + s)
            for k in blocks:
                terms = [own_rows(meta, sums, yh, z, 5 + s, k), yr[n, k]]
                if s > 0:
                    terms.append(al[s, k])
                al[s, k] = total(*terms).astype(BF)
            down_copy = links.send(al.at[s], al.at[s + 1], down)
        yield
    n = NEED.index(0)
    for k in blocks:
        agg[pl.ds(k * B, B), pl.ds(h * B, B)] = total(
            own_rows(meta, sums, yh, z, 0, k), yr[n, k], ar[4, k], al[3, k]
        ).astype(BF)


def reduce_rep_b(links, meta, sums, br, bl, by, agg, h):
    yh, z, x, yl, c = place()
    up, down = device(yh, rem(z + 1, NZ), x, yl, c), device(yh, rem(z + NZ - 1, NZ), x, yl, c)
    over = device(1 - yh, z, x, yl, c)
    sides = (yh, 1 - yh)
    first = A_BLOCKS[h]
    blocks = range(4 - first)
    up_copy = down_copy = None
    for s in range(5):
        if s > 0:
            down_copy.wait_recv()
        if s < 4:
            for n in range(2):
                for k in blocks:
                    terms = [own_rows(meta, sums, sides[n], z, 4 + s, first + k)]
                    if s > 0:
                        terms.append(bl[s, n, k])
                    bl[s, n, k] = total(*terms).astype(BF)
            down_copy = links.send(bl.at[s], bl.at[s + 1], down)
        if s > 0 and s < 4:
            up_copy.wait_recv()
        if s < 3:
            for n in range(2):
                for k in blocks:
                    terms = [own_rows(meta, sums, sides[n], z, 3 - s, first + k)]
                    if s > 0:
                        terms.append(br[s, n, k])
                    br[s, n, k] = total(*terms).astype(BF)
            up_copy = links.send(br.at[s], br.at[s + 1], up)
        if s < 4:
            yield
    for k in blocks:
        by[0, k] = total(own_rows(meta, sums, 1 - yh, z, 0, first + k), bl[4, 1, k], br[3, 1, k]).astype(BF)
    y_copy = links.send(by.at[0], by.at[1], over)
    yield
    y_copy.wait_recv()
    for k in blocks:
        agg[pl.ds((first + k) * B, B), pl.ds(h * B, B)] = total(
            own_rows(meta, sums, yh, z, 0, first + k), bl[4, 0, k], br[3, 0, k], by[1, k]
        ).astype(BF)


def gather_rep_a(links, panel, h):
    yh, z, x, yl, c = place()
    up, down = device(yh, rem(z + 1, NZ), x, yl, c), device(yh, rem(z + NZ - 1, NZ), x, yl, c)
    over = device(1 - yh, z, x, yl, c)

    def at(o):
        return panel.at[pl.ds((yh * 8 + rem(z + NZ + o, NZ)) * 4, A_BLOCKS[h])]

    up_copy = links.send(at(0), at(0), up)
    down_copy = links.send(at(0), at(0), down)
    y_copies = [links.send(at(0), at(0), over)]
    yield
    for s in range(1, 5):
        up_copy.wait_recv()
        if s < 4:
            up_copy = links.send(at(-s), at(-s), up)
        y_copies.append(links.send(at(-s), at(-s), over))
        if s < 4:
            down_copy.wait_recv()
            if s < 3:
                down_copy = links.send(at(s), at(s), down)
            y_copies.append(links.send(at(s), at(s), over))
        yield
    for copy in y_copies:
        copy.wait_recv()


def gather_rep_b(links, panel, h):
    yh, z, x, yl, c = place()
    up, down = device(yh, rem(z + 1, NZ), x, yl, c), device(yh, rem(z + NZ - 1, NZ), x, yl, c)
    over = device(1 - yh, z, x, yl, c)
    first = A_BLOCKS[h]

    def at(side, o):
        return panel.at[pl.ds((side * 8 + rem(z + NZ + o, NZ)) * 4 + first, 4 - first)]

    y_copy = links.send(at(yh, 0), at(yh, 0), over)
    ups, downs = [None, None], [None, None]
    sides = (yh, 1 - yh)
    for s in range(0, 5):
        for n in range(2):
            if s == 0 and n == 1:
                yield
                y_copy.wait_recv()
            if s > 0:
                downs[n].wait_recv()
            if s < 4:
                downs[n] = links.send(at(sides[n], s), at(sides[n], s), down)
            if s > 0 and s < 4:
                ups[n].wait_recv()
            if s < 3:
                ups[n] = links.send(at(sides[n], -s), at(sides[n], -s), up)
        if s < 4:
            yield


ORDER = ((2, 1), (2, 0), (1, 1), (3, 1), (1, 0), (3, 0), (0, 1), (0, 0))


def reduce_row(links, meta, sums, cs, cr, stage, got, result, h):
    yh, z, x, yl, c = place()
    right, left = device(yh, z, rem(x + 1, 4), yl, c), device(yh, z, rem(x + 3, 4), yl, c)
    over_y, sibling = device(yh, z, x, 1 - yl, c), device(yh, z, x, yl, 1 - c)

    def own(core, dx, other, k):
        side = 1 - yl if other else yl
        q = (rem(x + dx, 4) * 4 + side * 2 + core) * 4 + k
        return sums[meta[13, q]]

    core_copies = []
    for g in range(4):
        for n in (2 * g, 2 * g + 1):
            for k in range(4):
                cs[n, k] = own(1 - c, *ORDER[n], k)
        part = pl.ds(2 * g, 2)
        core_copies.append(links.send(cs.at[part], cr.at[part], sibling))

    def both(dx, other, k):
        return (own(c, dx, other, k), cr[ORDER.index((dx, other)), k])

    slots = []

    def push(to, dx, other, blocks, *more):
        n = len(slots)
        slots.append(None)
        for at, k in enumerate(blocks):
            extra = [f(k) for f in more]
            stage[n, at] = total(*both(dx, other, k), *[e for e in extra if e is not None]).astype(BF)
        part = pl.ds(0, len(blocks))
        slots[n] = links.send(stage.at[n, part], got.at[n, part], to)
        return n

    def arrived(n, blocks):
        return lambda k: got[n, blocks.index(k)] if k in blocks else None

    lower, upper = (0, 1), (2, 3)
    yield
    core_copies[0].wait_recv()
    p_y2 = push(over_y, 2, 1, lower)
    q_r1 = push(right, 2, 0, upper)
    q_l1 = push(left, 2, 1, upper)
    core_copies[1].wait_recv()
    p_y1 = push(over_y, 1, 1, lower)
    p_y3 = push(over_y, 3, 1, lower)
    q_rp = push(right, 1, 1, upper)
    core_copies[2].wait_recv()
    q_lo = push(left, 3, 0, upper)
    core_copies[3].wait_recv()
    p_y0 = push(over_y, 0, 1, lower)
    yield
    slots[p_y2].wait_recv()
    p_r1 = push(right, 2, 0, (0,), arrived(p_y2, lower))
    p_l1 = push(left, 2, 0, (1,), arrived(p_y2, lower))
    slots[q_r1].wait_recv()
    q_r2 = push(right, 1, 0, upper, arrived(q_r1, upper))
    slots[q_l1].wait_recv()
    q_l2 = push(left, 3, 1, upper, arrived(q_l1, upper))
    yield
    slots[p_y1].wait_recv()
    slots[p_y3].wait_recv()
    slots[p_r1].wait_recv()
    p_r2 = push(right, 1, 0, lower, arrived(p_y1, lower), arrived(p_r1, (0,)))
    slots[p_l1].wait_recv()
    p_l2 = push(left, 3, 0, lower, arrived(p_y3, lower), arrived(p_l1, (1,)))
    slots[q_rp].wait_recv()
    slots[q_l2].wait_recv()
    q_y = push(over_y, 0, 1, upper, arrived(q_rp, upper), arrived(q_l2, upper))
    yield
    for n in (p_y0, p_r2, p_l2):
        slots[n].wait_recv()

    def finish(k, *terms):
        result[pl.ds(k * B, B), pl.ds(h * B, B)] = total(*both(0, 0, k), *terms).T.astype(BF)

    for k in lower:
        finish(k, got[p_y0, k], got[p_r2, k], got[p_l2, k])
    for n in (q_lo, q_r2, q_y):
        slots[n].wait_recv()
    for k in upper:
        finish(k, got[q_lo, k - 2], got[q_r2, k - 2], got[q_y, k - 2])


def reduce_weight(links, pieces, core_in, x_in, y_in, z_in, s1, s2, out):
    yh, z, x, yl, c = place()
    y = yh * 2 + yl
    sibling = device(yh, z, x, yl, 1 - c)
    up, down = device(yh, rem(z + 1, NZ), x, yl, c), device(yh, rem(z + NZ - 1, NZ), x, yl, c)
    other_x = [rem(x + d, 4) for d in range(1, 4)]
    other_y = [(yh, 1 - yl), (1 - yh, yl), (1 - yh, 1 - yl)]

    copy = links.send(pieces.at[pl.ds((1 - c) * 16, 16)], core_in, sibling)
    yield
    copy.wait_recv()
    s1[...] = pieces[pl.ds(c * 16, 16)] + core_in[...]
    copies = [links.send(s1.at[pl.ds(to * 4, 4)], x_in.at[n], device(yh, z, to, yl, c)) for n, to in enumerate(other_x)]
    yield
    for copy in copies:
        copy.wait_recv()
    s2[...] = s1[pl.ds(x * 4, 4)] + x_in[0] + x_in[1] + x_in[2]
    copies = [links.send(s2.at[a * 2 + b], y_in.at[n], device(a, z, x, b, c)) for n, (a, b) in enumerate(other_y)]
    yield
    for copy in copies:
        copy.wait_recv()
    z_in[z] = s2[y] + y_in[0] + y_in[1] + y_in[2]
    up_copy = links.send(z_in.at[z], z_in.at[z], up)
    down_copy = links.send(z_in.at[z], z_in.at[z], down)
    for s in range(1, 5):
        yield
        up_copy.wait_recv()
        if s < 4:
            spot = rem(z + NZ - s, NZ)
            up_copy = links.send(z_in.at[spot], z_in.at[spot], up)
            down_copy.wait_recv()
        if s < 3:
            spot = rem(z + s, NZ)
            down_copy = links.send(z_in.at[spot], z_in.at[spot], down)
    summed = z_in[0]
    for n in range(1, NZ):
        summed = summed + z_in[n]
    spot = c * 16 + x * 4 + y
    out[spot] = summed
    copies = [links.send(out.at[spot], out.at[spot], device(a, z, x, b, c)) for a, b in other_y]
    yield
    for copy in copies:
        copy.wait_recv()
    part = out.at[pl.ds(c * 16 + x * 4, 4)]
    copies = [links.send(part, part, device(yh, z, to, yl, c)) for to in other_x]
    yield
    for copy in copies:
        copy.wait_recv()
    part = out.at[pl.ds(c * 16, 16)]
    copy = links.send(part, part, sibling)
    yield
    copy.wait_recv()


A_BLOCKS = (3, 2)
COPIES = 256


def half_scratch(a):
    b = 4 - a
    forward = [
        (RB, B, B), (PAIRS + 1, B, B), (8, a, B, B), (8, a, B, B), (5, a, B, B), (4, a, B, B),
        (4, 2, b, B, B), (5, 2, b, B, B), (2, b, B, B),
    ]
    backward = [(RB, B, B), (8, 4, B, B), (8, 4, B, B), (15, 2, B, B), (15, 2, B, B)]
    return forward + backward


PIECES = [
    (32, 8, 384), (16, 8, 384), (3, 4, 8, 384), (3, 8, 384), (8, 8, 384), (16, 8, 384), (4, 8, 384), (32, 8, 384),
]


def layer_kernel(meta, feat_hbm, cot_hbm, weight, bias, adj_hbm, act, result, gw, gb, adj, *rest):
    halves = [rest[:14], rest[14:28]]
    piece_refs, (agg, grad, feat, cot, send_sem, recv_sem, local_sem) = rest[28:36], rest[36:]
    yh, z, x, yl, c = place()
    barrier = pltpu.get_barrier_semaphore()
    partners = [
        device(yh, rem(z + 1, NZ), x, yl, c), device(yh, rem(z + NZ - 1, NZ), x, yl, c),
        device(1 - yh, z, x, yl, c), device(yh, z, rem(x + 1, 4), yl, c), device(yh, z, rem(x + 3, 4), yl, c),
        device(yh, z, rem(x + 2, 4), yl, c), device(yh, z, x, 1 - yl, c), device(yh, z, x, yl, 1 - c),
        device(1 - yh, z, x, 1 - yl, c),
    ]
    for to in partners:
        pl.semaphore_signal(barrier, inc=1, device_id=to, device_id_type=MESH)
    links = Links(send_sem, recv_sem)
    feat_copy = pltpu.make_async_copy(feat_hbm, feat, local_sem.at[0])
    feat_copy.start()
    adj_copy = pltpu.make_async_copy(adj_hbm, adj.at[pl.ds(0, CAP)], local_sem.at[1])
    adj_copy.start()
    cot_copy = pltpu.make_async_copy(cot_hbm, cot, local_sem.at[2])
    cot_copy.start()
    adj[CAP] = jnp.zeros((B, B), BF)
    slot = (c * 8 + x * 2 + yl) * 4
    feat_copy.wait()
    for h in range(2):
        for k in range(4):
            halves[h][0][slot + k] = feat[pl.ds(k * B, B), pl.ds(h * B, B)]
    pl.semaphore_wait(barrier, len(partners))

    def reduces(h):
        panel, sums, ys, yr, ar, al, br, bl, by = halves[h][:9]
        return (
            reduce_rep_b(links, meta, sums, br, bl, by, agg, h),
            reduce_rep_a(links, meta, sums, ys, yr, ar, al, agg, h),
        )

    first, second = gather_row_first(links, halves[0][0]), gather_row(links, halves[1][0])
    advance(first, 3)
    next(second)
    run(first)
    adj_copy.wait()
    cot_copy.wait()
    work = products(meta, 0, adj, halves[0][0], halves[0][1], True)
    for n in range(8):
        next(work)
        if n == 1:
            next(second)
    b0, a0 = reduces(0)
    next(a0)
    next(b0)
    run(second)
    work = products(meta, 0, adj, halves[1][0], halves[1][1], True)
    for n in range(8):
        next(work)
        if n in (2, 6):
            next(b0)
        if n == 4:
            next(a0)
    b1, a1 = reduces(1)
    next(a1)
    next(b1)
    run(a0, b0, b1, a1)

    spot = (yh * 8 + z) * 4
    for k in range(4):
        rows = pl.ds(k * B, B)
        pre = jnp.dot(agg[rows, :], weight[...], preferred_element_type=F32) + bias[...]
        s = jax.nn.sigmoid(pre)
        act[rows, :] = (pre * s).astype(BF)
        grad_pre = (cot[rows, :].astype(F32) * (s * (1.0 + pre * (1.0 - s)))).astype(BF)
        grad[rows, :] = grad_pre
        back = lax.dot_general(weight[...], grad_pre, (((1,), (1,)), ((), ())), preferred_element_type=F32).astype(BF)
        for h in range(2):
            halves[h][9][spot + k] = back[h * B : (h + 1) * B]
    first, second = [
        together(gather_rep_b(links, halves[h][9], h), gather_rep_a(links, halves[h][9], h)) for h in range(2)
    ]
    advance(first, 2)
    gw_local = lax.dot_general(agg[...], grad[...], (((0,), (0,)), ((), ())), preferred_element_type=F32)
    gb_local = jnp.sum(grad[...].astype(F32), axis=0, keepdims=True)
    row = lax.broadcasted_iota(jnp.int32, (8, B), 0)
    bias_tile = jnp.where(row == 0, gb_local[:, :B], jnp.where(row == 1, gb_local[:, B:], 0.0))
    pieces, out = piece_refs[0], piece_refs[7]
    for n in range(32):
        pieces[n, :, 0:256] = gw_local[n * 8 : n * 8 + 8]
        pieces[n, :, 256:384] = bias_tile
    weights = reduce_weight(links, *piece_refs)
    next(weights)
    advance(first, 2)
    advance(second, 2)
    for n in range(7):
        next(first, None)
        if n in (1, 4):
            next(weights)
        if n in (3, 5):
            next(second)
    run(first)
    work = products(meta, 8, adj, halves[0][9], halves[0][1], False)
    for n in range(8):
        next(work)
        if n % 2 == 1:
            next(second)
        if n == 3:
            next(weights)

    def row_sums(h):
        return reduce_row(links, meta, halves[h][1], *halves[h][10:14], result, h)

    first = row_sums(0)
    next(first)
    next(second, None)
    next(first)
    next(weights)
    next(second, None)
    next(weights)
    next(second, None)
    next(first)
    run(second)
    next(weights)
    work = products(meta, 8, adj, halves[1][9], halves[1][1], False)
    for n in range(8):
        next(work)
        if n == 1:
            next(first, None)
        if n in (3, 6):
            next(weights)
    second = row_sums(1)
    run(second, weights, first)
    for n in range(32):
        gw[n * 8 : n * 8 + 8, :] = out[n, :, 0:256]
    gb[:, 0:B] = out[0, 0:1, 256:384]
    gb[:, B:256] = out[0, 1:2, 256:384]
    links.finish()


def layer(meta, feat, cot, weight, bias, adj):
    vmem = pl.BlockSpec(memory_space=pltpu.VMEM)
    anywhere = pl.BlockSpec(memory_space=pl.ANY)
    return pl.pallas_call(
        layer_kernel,
        out_shape=OUTS,
        in_specs=[pl.BlockSpec(memory_space=pltpu.SMEM), anywhere, anywhere, vmem, vmem, anywhere],
        out_specs=(vmem, vmem, vmem, vmem),
        scratch_shapes=[pltpu.VMEM((CAP + 1, B, B), BF)]
        + [pltpu.VMEM(shape, BF) for a in A_BLOCKS for shape in half_scratch(a)]
        + [pltpu.VMEM(shape, F32) for shape in PIECES]
        + [
            pltpu.VMEM((512, 256), BF),
            pltpu.VMEM((512, 256), BF),
            pltpu.VMEM((512, 256), BF),
            pltpu.VMEM((512, 256), BF),
            pltpu.SemaphoreType.DMA((COPIES,)),
            pltpu.SemaphoreType.DMA((COPIES,)),
            pltpu.SemaphoreType.DMA((3,)),
        ],
        compiler_params=pltpu.CompilerParams(collective_id=1, has_side_effects=True, vmem_limit_bytes=VMEM_LIMIT),
    )(meta, feat, cot, weight, bias, adj)


OUTS = (
    jax.ShapeDtypeStruct((512, 256), BF),
    jax.ShapeDtypeStruct((512, 256), BF),
    jax.ShapeDtypeStruct((256, 256), F32),
    jax.ShapeDtypeStruct((1, 256), F32),
)


def hand_over_kernel(*refs):
    given, results, held, sem = refs[:4], refs[4:8], refs[8:12], refs[12]
    arrive = [pltpu.make_async_copy(given[n], held[n], sem.at[n]) for n in range(4)]
    leave = [pltpu.make_async_copy(held[n], results[n], sem.at[4 + n]) for n in range(4)]
    for copy in arrive:
        copy.start()
    for n in range(4):
        arrive[n].wait()
        leave[n].start()
    for copy in leave:
        copy.wait()


def hand_over(*arrays):
    outside = pl.BlockSpec(memory_space=pltpu.HBM)
    return pl.pallas_call(
        hand_over_kernel,
        out_shape=OUTS,
        in_specs=[outside] * 4,
        out_specs=(outside,) * 4,
        scratch_shapes=[pltpu.VMEM(out.shape, out.dtype) for out in OUTS] + [pltpu.SemaphoreType.DMA((8,))],
    )(*arrays)


def per_device(features, adj_values, block_rows, block_cols, counts, weight, bias, cotangent):
    adj = adj_values.reshape(CAP, B, B)
    meta = sort_lists(counts, block_rows.reshape(1, CAP), block_cols.reshape(1, CAP))
    act, result, gw, gb = hand_over(*layer(meta, features, cotangent, weight, bias.reshape(1, 256), adj))
    return act, result, gw, gb.reshape(256)


def solution(mesh):
    return jax.shard_map(
        per_device,
        mesh=mesh,
        in_specs=(
            P(("rep", "row"), None),
            P("rep", "row", None, None, None),
            P("rep", "row", None),
            P("rep", "row", None),
            P("rep", "row"),
            P(),
            P(),
            P(("rep", "row"), None),
        ),
        out_specs=(P(("rep", "row"), None), P(("rep", "row"), None), P(), P()),
        check_vma=False,
    )
```

```python
import functools

import jax
import jax.numpy as jnp
from jax import lax
from jax.experimental import pallas as pl
from jax.experimental.pallas import tpu as pltpu
from jax.sharding import PartitionSpec as P

MESH = pl.DeviceIdType.MESH
BF = jnp.bfloat16
F32 = jnp.float32
B = 128
CAP = 256
RB = 64
PAIRS = 160
NZ = 8
UNROLL = 20
VMEM_LIMIT = 58 * 2**20


def rem(a, n):
    return lax.rem(a, n)


def place():
    r = lax.axis_index("rep")
    i = lax.axis_index("row")
    return lax.div(r, 8), rem(r, 8), lax.div(i, 4), rem(lax.div(i, 2), 2), rem(i, 2)


def device(yh, z, x, yl, c):
    return (yh * 8 + z, x * 4 + yl * 2 + c)


class Links:
    def __init__(self, send_sem, recv_sem):
        self.send_sem, self.recv_sem, self.copies = send_sem, recv_sem, []

    def send(self, src, dst, to):
        k = len(self.copies)
        copy = pltpu.make_async_remote_copy(
            src_ref=src, dst_ref=dst, send_sem=self.send_sem.at[k], recv_sem=self.recv_sem.at[k],
            device_id=to, device_id_type=MESH,
        )
        copy.start()
        self.copies.append(copy)
        return copy

    def finish(self):
        for copy in self.copies:
            copy.wait_send()


def run(*tasks):
    tasks = list(tasks)
    while tasks:
        for task in list(tasks):
            if next(task, "end") == "end":
                tasks.remove(task)


def together(*tasks):
    tasks = list(tasks)
    while tasks:
        for task in list(tasks):
            if next(task, "end") == "end":
                tasks.remove(task)
            else:
                yield


def advance(task, n):
    for _ in range(n):
        next(task, None)


def entry(meta, row, n, top):
    return jnp.minimum(jnp.maximum(meta[row, n], 0), top)


def products(meta, base, adj, source, sums, adj_first):
    def step(t, acc):
        a0, a1 = adj[entry(meta, base, t, CAP)], adj[entry(meta, base + 1, t, CAP)]
        x0, x1 = source[entry(meta, base + 2, t, RB - 1)], source[entry(meta, base + 3, t, RB - 1)]
        if adj_first:
            left, right = jnp.concatenate([a0, a1], 1), jnp.concatenate([x0, x1], 0)
        else:
            left, right = jnp.concatenate([x0, x1], 1), jnp.concatenate([a0, a1], 0)
        term = jnp.dot(left, right, preferred_element_type=F32)
        acc = jnp.where(meta[base + 4, t] != 0, 0.0, acc) + term
        sums[t] = acc.astype(BF)
        return acc

    def group(g, acc):
        for k in range(UNROLL):
            acc = step(g * UNROLL + k, acc)
        return acc

    acc = jnp.zeros((B, B), F32)
    sums[PAIRS] = jnp.zeros((B, B), BF)
    for g in range(PAIRS // UNROLL):
        acc = lax.fori_loop(g, g + 1, group, acc)
        yield


def sort_lists(count_ref, rows_ref, cols_ref, out_ref):
    live = (lax.broadcasted_iota(jnp.int32, (1, CAP), 1) < count_ref[0, 0]).astype(F32)
    sub = lax.broadcasted_iota(jnp.int32, (CAP, CAP), 0).astype(F32)
    lane = lax.broadcasted_iota(jnp.int32, (CAP, CAP), 1).astype(F32)
    eye = (sub == lane).astype(F32)
    rows = rows_ref[...].astype(F32)
    cols = cols_ref[...].astype(F32)

    def column(v):
        return jnp.sum(eye * v, axis=1, keepdims=True)

    def order(key, source):
        key = jnp.where(live > 0, key, 64.0)
        key_col = column(key)
        same = jnp.where(key_col == key, 1.0, 0.0)
        rank = jnp.sum(jnp.where(sub < lane, same, 0.0), axis=0, keepdims=True)
        p = sub[:RB]
        n = jnp.sum(jnp.where(p == key, 1.0, 0.0), axis=1, keepdims=True)
        pairs = jnp.floor((n + 1.0) * 0.5)
        base = jnp.sum(jnp.where(p < key, pairs, 0.0), axis=0, keepdims=True)
        slot = jnp.where(live > 0, 2.0 * base + rank, -1.0)
        slot_col = column(slot)
        first_hot = jnp.where(slot_col == 2.0 * lane, 1.0, 0.0)
        second_hot = jnp.where(slot_col == 2.0 * lane + 1.0, 1.0, 0.0)
        source_col = column(source)
        fresh_col = column(jnp.where(rank == 0.0, 1.0, 0.0))

        def pick(hot, v):
            return jnp.sum(hot * v, axis=0, keepdims=True)

        entry = sub[:, :1]
        a0 = pick(first_hot, entry - CAP) + CAP
        a1 = pick(second_hot, entry - CAP) + CAP
        before = jnp.sum(jnp.where(p < lane[:RB], pairs, 0.0), axis=0, keepdims=True)
        mine = jnp.sum(jnp.where(p == lane[:RB], pairs, 0.0), axis=0, keepdims=True)
        last = jnp.where(mine > 0, before + mine - 1.0, float(PAIRS))
        zero = jnp.zeros((1, CAP), F32)
        return [a0, a1, pick(first_hot, source_col), pick(second_hot, source_col), pick(first_hot, fresh_col), last, zero, zero]

    i = jnp.floor(cols * 0.25)
    x = jnp.floor(i * 0.25)
    yl = jnp.floor((i - 4.0 * x) * 0.5)
    c = i - 4.0 * x - 2.0 * yl
    col_place = (c * 8.0 + x * 2.0 + yl) * 4.0 + (cols - 4.0 * i)
    table = order(rows, col_place) + order(cols, rows)
    out_ref[...] = jnp.concatenate(table, axis=0).astype(jnp.int32)


def gather_row_first(links, panel):
    yh, z, x, yl, c = place()
    xp, xm, xf, yo = rem(x + 1, 4), rem(x + 3, 4), rem(x + 2, 4), 1 - yl

    def at(at_x, at_y, first, n):
        return panel.at[pl.ds((c * 8 + at_x * 2 + at_y) * 4 + first, n)]

    over_y, sibling = device(yh, z, x, yo, c), device(yh, z, x, yl, 1 - c)
    around = [device(yh, z, xp, yl, c), device(yh, z, xm, yl, c), device(yh, z, xf, yl, c)]
    origin = (xm, xp, xf)

    def send(at_x, at_y, first, n, to):
        ref = at(at_x, at_y, first, n)
        return links.send(ref, ref, to)

    y_lo = send(x, yl, 0, 2, over_y)
    hi = [send(x, yl, 2, 2, to) for to in around]
    y_hi = send(x, yl, 2, 2, over_y)
    lo = [send(x, yl, 0, 2, to) for to in around]
    to_core = [send(x, yl, 0, 4, sibling)]
    yield
    y_lo.wait_recv()
    lo_other = [send(x, yo, 0, 2, to) for to in around]
    hi_other = []
    for n in range(3):
        hi[n].wait_recv()
        hi_other.append(send(origin[n], yl, 2, 2, over_y))
    yield
    y_hi.wait_recv()
    to_core.append(send(x, yo, 0, 4, sibling))
    for n in range(3):
        lo[n].wait_recv()
        to_core.append(send(origin[n], yl, 0, 4, sibling))
    yield
    for n in range(3):
        lo_other[n].wait_recv()
        hi_other[n].wait_recv()
        to_core.append(send(origin[n], yo, 0, 4, sibling))
    yield
    for copy in to_core:
        copy.wait_recv()


def gather_row(links, panel):
    yh, z, x, yl, c = place()
    xp, xm, yo, co = rem(x + 1, 4), rem(x + 3, 4), 1 - yl, 1 - c

    def one(at_x, at_y):
        return panel.at[pl.ds((c * 8 + at_x * 2 + at_y) * 4, 4)]

    def two(at_x):
        return panel.at[pl.ds((c * 8 + at_x * 2) * 4, 8)]

    right, left = device(yh, z, xp, yl, c), device(yh, z, xm, yl, c)
    over_y, sibling = device(yh, z, x, yo, c), device(yh, z, x, yl, co)
    mine, other = one(x, yl), one(x, yo)
    y_copy = links.send(mine, mine, over_y)
    r_mine = links.send(mine, mine, right)
    l_mine = links.send(mine, mine, left)
    to_core = [links.send(mine, mine, sibling)]
    yield
    y_copy.wait_recv()
    r_other = links.send(other, other, right)
    l_other = links.send(other, other, left)
    to_core.append(links.send(other, other, sibling))
    r_mine.wait_recv()
    r_far = links.send(one(xm, yl), one(xm, yl), right)
    yield
    l_other.wait_recv()
    l_far = links.send(one(xp, yo), one(xp, yo), left)
    r_other.wait_recv()
    to_core.append(links.send(two(xm), two(xm), sibling))
    l_mine.wait_recv()
    to_core.append(links.send(two(xp), two(xp), sibling))
    yield
    far = rem(x + 2, 4)
    r_far.wait_recv()
    to_core.append(links.send(one(far, yl), one(far, yl), sibling))
    l_far.wait_recv()
    to_core.append(links.send(one(far, yo), one(far, yo), sibling))
    yield
    for copy in to_core:
        copy.wait_recv()


def total(*terms):
    out = terms[0].astype(F32)
    for term in terms[1:]:
        out = out + term.astype(F32)
    return out


def own_rows(meta, sums, yh, z, o, block):
    p = (yh * 8 + rem(z + o, NZ)) * 4 + block
    return sums[entry(meta, 5, p, PAIRS)]


NEED = (4, 5, 3, 6, 2, 7, 1, 0)


def reduce_rep_a(links, meta, sums, ys, yr, ar, al, agg, h):
    yh, z, x, yl, c = place()
    up, down = device(yh, rem(z + 1, NZ), x, yl, c), device(yh, rem(z + NZ - 1, NZ), x, yl, c)
    over = device(1 - yh, z, x, yl, c)
    blocks = range(A_BLOCKS[h])
    y_copies = []
    for g in range(4):
        for n in (2 * g, 2 * g + 1):
            for k in blocks:
                ys[n, k] = own_rows(meta, sums, 1 - yh, z, NEED[n], k)
        part = pl.ds(2 * g, 2)
        y_copies.append(links.send(ys.at[part], yr.at[part], over))
    yield
    up_copy = down_copy = None
    for s in range(5):
        if s < 4:
            y_copies[s].wait_recv()
        if s > 0:
            up_copy.wait_recv()
        if s < 4:
            n = NEED.index(4 - s)
            for k in blocks:
                terms = [own_rows(meta, sums, yh, z, 4 - s, k), yr[n, k]]
                if s > 0:
                    terms.append(ar[s, k])
                ar[s, k] = total(*terms).astype(BF)
            up_copy = links.send(ar.at[s], ar.at[s + 1], up)
        if s > 0 and s < 4:
            down_copy.wait_recv()
        if s < 3:
            n = NEED.index(5 + s)
            for k in blocks:
                terms = [own_rows(meta, sums, yh, z, 5 + s, k), yr[n, k]]
                if s > 0:
                    terms.append(al[s, k])
                al[s, k] = total(*terms).astype(BF)
            down_copy = links.send(al.at[s], al.at[s + 1], down)
        yield
    n = NEED.index(0)
    for k in blocks:
        agg[pl.ds(k * B, B), pl.ds(h * B, B)] = total(
            own_rows(meta, sums, yh, z, 0, k), yr[n, k], ar[4, k], al[3, k]
        ).astype(BF)


def reduce_rep_b(links, meta, sums, br, bl, by, agg, h):
    yh, z, x, yl, c = place()
    up, down = device(yh, rem(z + 1, NZ), x, yl, c), device(yh, rem(z + NZ - 1, NZ), x, yl, c)
    over = device(1 - yh, z, x, yl, c)
    sides = (yh, 1 - yh)
    first = A_BLOCKS[h]
    blocks = range(4 - first)
    up_copy = down_copy = None
    for s in range(5):
        if s > 0:
            down_copy.wait_recv()
        if s < 4:
            for n in range(2):
                for k in blocks:
                    terms = [own_rows(meta, sums, sides[n], z, 4 + s, first + k)]
                    if s > 0:
                        terms.append(bl[s, n, k])
                    bl[s, n, k] = total(*terms).astype(BF)
            down_copy = links.send(bl.at[s], bl.at[s + 1], down)
        if s > 0 and s < 4:
            up_copy.wait_recv()
        if s < 3:
            for n in range(2):
                for k in blocks:
                    terms = [own_rows(meta, sums, sides[n], z, 3 - s, first + k)]
                    if s > 0:
                        terms.append(br[s, n, k])
                    br[s, n, k] = total(*terms).astype(BF)
            up_copy = links.send(br.at[s], br.at[s + 1], up)
        if s < 4:
            yield
    for k in blocks:
        by[0, k] = total(own_rows(meta, sums, 1 - yh, z, 0, first + k), bl[4, 1, k], br[3, 1, k]).astype(BF)
    y_copy = links.send(by.at[0], by.at[1], over)
    yield
    y_copy.wait_recv()
    for k in blocks:
        agg[pl.ds((first + k) * B, B), pl.ds(h * B, B)] = total(
            own_rows(meta, sums, yh, z, 0, first + k), bl[4, 0, k], br[3, 0, k], by[1, k]
        ).astype(BF)


def gather_rep_a(links, panel, h):
    yh, z, x, yl, c = place()
    up, down = device(yh, rem(z + 1, NZ), x, yl, c), device(yh, rem(z + NZ - 1, NZ), x, yl, c)
    over = device(1 - yh, z, x, yl, c)

    def at(o):
        return panel.at[pl.ds((yh * 8 + rem(z + NZ + o, NZ)) * 4, A_BLOCKS[h])]

    up_copy = links.send(at(0), at(0), up)
    down_copy = links.send(at(0), at(0), down)
    y_copies = [links.send(at(0), at(0), over)]
    yield
    for s in range(1, 5):
        up_copy.wait_recv()
        if s < 4:
            up_copy = links.send(at(-s), at(-s), up)
        y_copies.append(links.send(at(-s), at(-s), over))
        if s < 4:
            down_copy.wait_recv()
            if s < 3:
                down_copy = links.send(at(s), at(s), down)
            y_copies.append(links.send(at(s), at(s), over))
        yield
    for copy in y_copies:
        copy.wait_recv()


def gather_rep_b(links, panel, h):
    yh, z, x, yl, c = place()
    up, down = device(yh, rem(z + 1, NZ), x, yl, c), device(yh, rem(z + NZ - 1, NZ), x, yl, c)
    over = device(1 - yh, z, x, yl, c)
    first = A_BLOCKS[h]

    def at(side, o):
        return panel.at[pl.ds((side * 8 + rem(z + NZ + o, NZ)) * 4 + first, 4 - first)]

    y_copy = links.send(at(yh, 0), at(yh, 0), over)
    ups, downs = [None, None], [None, None]
    sides = (yh, 1 - yh)
    for s in range(0, 5):
        for n in range(2):
            if s == 0 and n == 1:
                yield
                y_copy.wait_recv()
            if s > 0:
                downs[n].wait_recv()
            if s < 4:
                downs[n] = links.send(at(sides[n], s), at(sides[n], s), down)
            if s > 0 and s < 4:
                ups[n].wait_recv()
            if s < 3:
                ups[n] = links.send(at(sides[n], -s), at(sides[n], -s), up)
        if s < 4:
            yield


ORDER = ((2, 1), (2, 0), (1, 1), (3, 1), (1, 0), (3, 0), (0, 1), (0, 0))


def reduce_row(links, meta, sums, cs, cr, stage, got, result, h):
    yh, z, x, yl, c = place()
    right, left = device(yh, z, rem(x + 1, 4), yl, c), device(yh, z, rem(x + 3, 4), yl, c)
    over_y, sibling = device(yh, z, x, 1 - yl, c), device(yh, z, x, yl, 1 - c)

    def own(core, dx, other, k):
        side = 1 - yl if other else yl
        q = (rem(x + dx, 4) * 4 + side * 2 + core) * 4 + k
        return sums[entry(meta, 13, q, PAIRS)]

    core_copies = []
    for g in range(4):
        for n in (2 * g, 2 * g + 1):
            for k in range(4):
                cs[n, k] = own(1 - c, *ORDER[n], k)
        part = pl.ds(2 * g, 2)
        core_copies.append(links.send(cs.at[part], cr.at[part], sibling))

    def both(dx, other, k):
        return (own(c, dx, other, k), cr[ORDER.index((dx, other)), k])

    slots = []

    def push(to, dx, other, blocks, *more):
        n = len(slots)
        slots.append(None)
        for at, k in enumerate(blocks):
            extra = [f(k) for f in more]
            stage[n, at] = total(*both(dx, other, k), *[e for e in extra if e is not None]).astype(BF)
        part = pl.ds(0, len(blocks))
        slots[n] = links.send(stage.at[n, part], got.at[n, part], to)
        return n

    def arrived(n, blocks):
        return lambda k: got[n, blocks.index(k)] if k in blocks else None

    lower, upper = (0, 1), (2, 3)
    yield
    core_copies[0].wait_recv()
    p_y2 = push(over_y, 2, 1, lower)
    q_r1 = push(right, 2, 0, upper)
    q_l1 = push(left, 2, 1, upper)
    core_copies[1].wait_recv()
    p_y1 = push(over_y, 1, 1, lower)
    p_y3 = push(over_y, 3, 1, lower)
    q_rp = push(right, 1, 1, upper)
    core_copies[2].wait_recv()
    q_lo = push(left, 3, 0, upper)
    core_copies[3].wait_recv()
    p_y0 = push(over_y, 0, 1, lower)
    yield
    slots[p_y2].wait_recv()
    p_r1 = push(right, 2, 0, (0,), arrived(p_y2, lower))
    p_l1 = push(left, 2, 0, (1,), arrived(p_y2, lower))
    slots[q_r1].wait_recv()
    q_r2 = push(right, 1, 0, upper, arrived(q_r1, upper))
    slots[q_l1].wait_recv()
    q_l2 = push(left, 3, 1, upper, arrived(q_l1, upper))
    yield
    slots[p_y1].wait_recv()
    slots[p_y3].wait_recv()
    slots[p_r1].wait_recv()
    p_r2 = push(right, 1, 0, lower, arrived(p_y1, lower), arrived(p_r1, (0,)))
    slots[p_l1].wait_recv()
    p_l2 = push(left, 3, 0, lower, arrived(p_y3, lower), arrived(p_l1, (1,)))
    slots[q_rp].wait_recv()
    slots[q_l2].wait_recv()
    q_y = push(over_y, 0, 1, upper, arrived(q_rp, upper), arrived(q_l2, upper))
    yield
    for n in (p_y0, p_r2, p_l2):
        slots[n].wait_recv()

    def finish(k, *terms):
        result[pl.ds(k * B, B), pl.ds(h * B, B)] = total(*both(0, 0, k), *terms).T.astype(BF)

    for k in lower:
        finish(k, got[p_y0, k], got[p_r2, k], got[p_l2, k])
    for n in (q_lo, q_r2, q_y):
        slots[n].wait_recv()
    for k in upper:
        finish(k, got[q_lo, k - 2], got[q_r2, k - 2], got[q_y, k - 2])


def reduce_weight(links, pieces, core_in, x_in, y_in, z_in, s1, s2, out):
    yh, z, x, yl, c = place()
    y = yh * 2 + yl
    sibling = device(yh, z, x, yl, 1 - c)
    up, down = device(yh, rem(z + 1, NZ), x, yl, c), device(yh, rem(z + NZ - 1, NZ), x, yl, c)
    other_x = [rem(x + d, 4) for d in range(1, 4)]
    other_y = [(yh, 1 - yl), (1 - yh, yl), (1 - yh, 1 - yl)]

    copy = links.send(pieces.at[pl.ds((1 - c) * 16, 16)], core_in, sibling)
    yield
    copy.wait_recv()
    s1[...] = pieces[pl.ds(c * 16, 16)] + core_in[...]
    copies = [links.send(s1.at[pl.ds(to * 4, 4)], x_in.at[n], device(yh, z, to, yl, c)) for n, to in enumerate(other_x)]
    yield
    for copy in copies:
        copy.wait_recv()
    s2[...] = s1[pl.ds(x * 4, 4)] + x_in[0] + x_in[1] + x_in[2]
    copies = [links.send(s2.at[a * 2 + b], y_in.at[n], device(a, z, x, b, c)) for n, (a, b) in enumerate(other_y)]
    yield
    for copy in copies:
        copy.wait_recv()
    z_in[z] = s2[y] + y_in[0] + y_in[1] + y_in[2]
    up_copy = links.send(z_in.at[z], z_in.at[z], up)
    down_copy = links.send(z_in.at[z], z_in.at[z], down)
    for s in range(1, 5):
        yield
        up_copy.wait_recv()
        if s < 4:
            spot = rem(z + NZ - s, NZ)
            up_copy = links.send(z_in.at[spot], z_in.at[spot], up)
            down_copy.wait_recv()
        if s < 3:
            spot = rem(z + s, NZ)
            down_copy = links.send(z_in.at[spot], z_in.at[spot], down)
    summed = z_in[0]
    for n in range(1, NZ):
        summed = summed + z_in[n]
    spot = c * 16 + x * 4 + y
    out[spot] = summed
    copies = [links.send(out.at[spot], out.at[spot], device(a, z, x, b, c)) for a, b in other_y]
    yield
    for copy in copies:
        copy.wait_recv()
    part = out.at[pl.ds(c * 16 + x * 4, 4)]
    copies = [links.send(part, part, device(yh, z, to, yl, c)) for to in other_x]
    yield
    for copy in copies:
        copy.wait_recv()
    part = out.at[pl.ds(c * 16, 16)]
    copy = links.send(part, part, sibling)
    yield
    copy.wait_recv()


A_BLOCKS = (3, 2)
COPIES = 256


def half_scratch(a):
    b = 4 - a
    forward = [
        (RB, B, B), (PAIRS + 1, B, B), (8, a, B, B), (8, a, B, B), (5, a, B, B), (4, a, B, B),
        (4, 2, b, B, B), (5, 2, b, B, B), (2, b, B, B),
    ]
    backward = [(RB, B, B), (8, 4, B, B), (8, 4, B, B), (15, 2, B, B), (15, 2, B, B)]
    return forward + backward


PIECES = [
    (32, 8, 384), (16, 8, 384), (3, 4, 8, 384), (3, 8, 384), (8, 8, 384), (16, 8, 384), (4, 8, 384), (32, 8, 384),
]


def layer_kernel(count, list_rows, list_cols, feat_hbm, cot_hbm, weight, bias, adj_hbm, act, result, gw, gb, adj, *rest):
    halves = [rest[:14], rest[14:28]]
    piece_refs, (agg, grad, feat, cot, table, meta, send_sem, recv_sem, local_sem) = rest[28:36], rest[36:]
    yh, z, x, yl, c = place()
    barrier = pltpu.get_barrier_semaphore()
    partners = [
        device(yh, rem(z + 1, NZ), x, yl, c), device(yh, rem(z + NZ - 1, NZ), x, yl, c),
        device(1 - yh, z, x, yl, c), device(yh, z, rem(x + 1, 4), yl, c), device(yh, z, rem(x + 3, 4), yl, c),
        device(yh, z, rem(x + 2, 4), yl, c), device(yh, z, x, 1 - yl, c), device(yh, z, x, yl, 1 - c),
        device(1 - yh, z, x, 1 - yl, c),
    ]
    for to in partners:
        pl.semaphore_signal(barrier, inc=1, device_id=to, device_id_type=MESH)
    links = Links(send_sem, recv_sem)
    feat_copy = pltpu.make_async_copy(feat_hbm, feat, local_sem.at[0])
    feat_copy.start()
    adj_copy = pltpu.make_async_copy(adj_hbm, adj.at[pl.ds(0, CAP)], local_sem.at[1])
    adj_copy.start()
    cot_copy = pltpu.make_async_copy(cot_hbm, cot, local_sem.at[2])
    cot_copy.start()
    adj[CAP] = jnp.zeros((B, B), BF)
    slot = (c * 8 + x * 2 + yl) * 4
    feat_copy.wait()
    for h in range(2):
        for k in range(4):
            halves[h][0][slot + k] = feat[pl.ds(k * B, B), pl.ds(h * B, B)]
    sort_lists(count, list_rows, list_cols, table)
    meta_copy = pltpu.make_async_copy(table, meta, local_sem.at[3])
    meta_copy.start()
    pl.semaphore_wait(barrier, len(partners))

    def reduces(h):
        panel, sums, ys, yr, ar, al, br, bl, by = halves[h][:9]
        return (
            reduce_rep_b(links, meta, sums, br, bl, by, agg, h),
            reduce_rep_a(links, meta, sums, ys, yr, ar, al, agg, h),
        )

    first, second = gather_row_first(links, halves[0][0]), gather_row(links, halves[1][0])
    advance(first, 3)
    next(second)
    run(first)
    meta_copy.wait()
    adj_copy.wait()
    cot_copy.wait()
    work = products(meta, 0, adj, halves[0][0], halves[0][1], True)
    for n in range(8):
        next(work)
        if n == 1:
            next(second)
    b0, a0 = reduces(0)
    next(a0)
    next(b0)
    run(second)
    work = products(meta, 0, adj, halves[1][0], halves[1][1], True)
    for n in range(8):
        next(work)
        if n in (2, 6):
            next(b0)
        if n == 4:
            next(a0)
    b1, a1 = reduces(1)
    next(a1)
    next(b1)
    run(a0, b0, b1, a1)

    spot = (yh * 8 + z) * 4
    for k in range(4):
        rows = pl.ds(k * B, B)
        pre = jnp.dot(agg[rows, :], weight[...], preferred_element_type=F32) + bias[...]
        s = jax.nn.sigmoid(pre)
        act[rows, :] = (pre * s).astype(BF)
        grad_pre = (cot[rows, :].astype(F32) * (s * (1.0 + pre * (1.0 - s)))).astype(BF)
        grad[rows, :] = grad_pre
        back = lax.dot_general(weight[...], grad_pre, (((1,), (1,)), ((), ())), preferred_element_type=F32).astype(BF)
        for h in range(2):
            halves[h][9][spot + k] = back[h * B : (h + 1) * B]
    first, second = [
        together(gather_rep_b(links, halves[h][9], h), gather_rep_a(links, halves[h][9], h)) for h in range(2)
    ]
    tasks = dict(F=first, S=second)

    def follow(order):
        for name in order:
            next(tasks[name], None)

    follow("FFSS")
    gw_local = lax.dot_general(agg[...], grad[...], (((0,), (0,)), ((), ())), preferred_element_type=F32)
    gb_local = jnp.sum(grad[...].astype(F32), axis=0, keepdims=True)
    row = lax.broadcasted_iota(jnp.int32, (8, B), 0)
    bias_tile = jnp.where(row == 0, gb_local[:, :B], jnp.where(row == 1, gb_local[:, B:], 0.0))
    pieces, out = piece_refs[0], piece_refs[7]
    for n in range(32):
        pieces[n, :, 0:256] = gw_local[n * 8 : n * 8 + 8]
        pieces[n, :, 256:384] = bias_tile

    def row_sums(h):
        return reduce_row(links, meta, halves[h][1], *halves[h][10:14], result, h)

    tasks["W"] = reduce_weight(links, *piece_refs)
    tasks["P"] = products(meta, 8, adj, halves[0][9], halves[0][1], False)
    tasks["R"] = row_sums(0)
    follow("WFFSWFFSSWFSFSWFSF")
    run(first)
    follow("PSPSWPSPSPPWPPRR")
    run(tasks["P"], second)
    tasks["P"] = products(meta, 8, adj, halves[1][9], halves[1][1], False)
    follow("WPPRPWPPRWPPRWP")
    run(tasks["P"])
    run(row_sums(1), tasks["W"], tasks["R"])
    for n in range(32):
        gw[n * 8 : n * 8 + 8, :] = out[n, :, 0:256]
    gb[:, 0:B] = out[0, 0:1, 256:384]
    gb[:, B:256] = out[0, 1:2, 256:384]
    links.finish()


def layer(count, rows, cols, feat, cot, weight, bias, adj):
    vmem = pl.BlockSpec(memory_space=pltpu.VMEM)
    anywhere = pl.BlockSpec(memory_space=pl.ANY)
    return pl.pallas_call(
        layer_kernel,
        out_shape=OUTS,
        in_specs=[pl.BlockSpec(memory_space=pltpu.SMEM), vmem, vmem, anywhere, anywhere, vmem, vmem, anywhere],
        out_specs=(vmem, vmem, vmem, vmem),
        scratch_shapes=[pltpu.VMEM((CAP + 1, B, B), BF)]
        + [pltpu.VMEM(shape, BF) for a in A_BLOCKS for shape in half_scratch(a)]
        + [pltpu.VMEM(shape, F32) for shape in PIECES]
        + [
            pltpu.VMEM((512, 256), BF),
            pltpu.VMEM((512, 256), BF),
            pltpu.VMEM((512, 256), BF),
            pltpu.VMEM((512, 256), BF),
            pltpu.VMEM((16, CAP), jnp.int32),
            pltpu.SMEM((16, CAP), jnp.int32),
            pltpu.SemaphoreType.DMA((COPIES,)),
            pltpu.SemaphoreType.DMA((COPIES,)),
            pltpu.SemaphoreType.DMA((4,)),
        ],
        compiler_params=pltpu.CompilerParams(collective_id=1, has_side_effects=True, vmem_limit_bytes=VMEM_LIMIT),
    )(count, rows, cols, feat, cot, weight, bias, adj)


OUTS = (
    jax.ShapeDtypeStruct((512, 256), BF),
    jax.ShapeDtypeStruct((512, 256), BF),
    jax.ShapeDtypeStruct((256, 256), F32),
    jax.ShapeDtypeStruct((1, 256), F32),
)


def hand_over_kernel(*refs):
    given, results, held, sem = refs[:4], refs[4:8], refs[8:12], refs[12]
    arrive = [pltpu.make_async_copy(given[n], held[n], sem.at[n]) for n in range(4)]
    leave = [pltpu.make_async_copy(held[n], results[n], sem.at[4 + n]) for n in range(4)]
    for copy in arrive:
        copy.start()
    for n in range(4):
        arrive[n].wait()
        leave[n].start()
    for copy in leave:
        copy.wait()


def hand_over(*arrays):
    outside = pl.BlockSpec(memory_space=pltpu.HBM)
    return pl.pallas_call(
        hand_over_kernel,
        out_shape=OUTS,
        in_specs=[outside] * 4,
        out_specs=(outside,) * 4,
        scratch_shapes=[pltpu.VMEM(out.shape, out.dtype) for out in OUTS] + [pltpu.SemaphoreType.DMA((8,))],
    )(*arrays)


def per_device(features, adj_values, block_rows, block_cols, counts, weight, bias, cotangent):
    adj = adj_values.reshape(CAP, B, B)
    rows, cols = block_rows.reshape(1, CAP), block_cols.reshape(1, CAP)
    act, result, gw, gb = hand_over(
        *layer(counts, rows, cols, features, cotangent, weight, bias.reshape(1, 256), adj)
    )
    return act, result, gw, gb.reshape(256)


def solution(mesh):
    return jax.shard_map(
        per_device,
        mesh=mesh,
        in_specs=(
            P(("rep", "row"), None),
            P("rep", "row", None, None, None),
            P("rep", "row", None),
            P("rep", "row", None),
            P("rep", "row"),
            P(),
            P(),
            P(("rep", "row"), None),
        ),
        out_specs=(P(("rep", "row"), None), P(("rep", "row"), None), P(), P()),
        check_vma=False,
    )
```
